32 devices in a mesh: dp: 4 (over y, x), ctx: 8 (over z, core).
Axes of the slice: x: 2, y: 2, z: 4, core: 2. Of those that a mesh axis runs over, the one named last changes fastest.
Arguments:
- queries: bfloat16 [2048, 4096], P(('dp', 'ctx')), parts along dimension 0, may hold values from -6 to 6
- keys: bfloat16 [2048, 4096], P(('dp', 'ctx')), parts along dimension 0, may hold values from -6 to 6
- values: bfloat16 [2048, 4096], P(('dp', 'ctx')), parts along dimension 0, may hold values from -6 to 6
- doc_starts: int32 [2048], P(('dp', 'ctx')), parts along dimension 0, may hold values from 0 to 1
- decay_exps: int32 [32], replicated, may hold values from 1 to 2047
- norm_gain: float32 [4096], replicated, may hold values from 0.25 to 1.75
Outputs:
- attended: bfloat16 [2048, 4096], P(('dp', 'ctx')), parts along dimension 0
The draws below stay inside these ranges and needn't reach their ends.
There are 4 independent parts, one for each index of `dp`. The reference program is written for one: setup_inputs(seed, part) draws one part's arguments, and reference() takes and returns one part's arrays. A program takes and returns all parts, laid end to end along the dimension named above; an argument that names none is the same for every part. Nothing has to cross between parts.
All inputs are finite; a program needn't handle non-finite values.
Results may differ from the reference program's by a relative error of at most 0.0053.
Values may be sent and summed in bfloat16 or wider, within the bound.
A program may use at most 192 MiB of HBM per device.

```python
import jax
import jax.numpy as jnp
from jax import lax

HEADS = 32
HEAD = 128
TOK_DEV = 64
TOKENS = 512


def draw_doc_starts(key, part):
    key_first = jax.random.fold_in(key, 11)
    key_last = jax.random.fold_in(key, 12)
    span = max(TOKENS // 8, 2)
    first_start = jax.random.randint(key_first, (), 1, span)
    last_start = jax.random.randint(key_last, (), TOKENS - span, TOKENS)
    places = jnp.arange(TOKENS)
    return jnp.where((places == first_start) | (places == last_start), 1, 0).astype(jnp.int32)


def draw_decay_exps(key, part):
    key_order = jax.random.fold_in(key, 21)
    key_extra = jax.random.fold_in(key, 22)
    order = jax.random.permutation(key_order, HEADS).astype(jnp.int32)
    shifts = order * 11 // HEADS
    base = jnp.left_shift(jnp.ones((HEADS,), jnp.int32), shifts)
    extra = jax.random.randint(key_extra, (HEADS,), 0, 1 << 20) % base
    value = base + extra
    value = jnp.where(order == HEADS - 1, 2047, value)
    value = jnp.where(order == 0, 1, value)
    return value.astype(jnp.int32)


def shard_levels(key, shape, pieces, smallest, high):
    level = 1.0
    for axis_at, parts in pieces:
        steps = jax.random.uniform(jax.random.fold_in(jax.random.fold_in(key, 6), axis_at), (parts,), jnp.float32, smallest / len(pieces), high / len(pieces))
        level = level * jnp.repeat(jnp.exp(steps), shape[axis_at] // parts).reshape((-1,) + (1,) * (len(shape) - 1 - axis_at))
    return level


def gaussian(own_key, extent, scale, limit, cuts=(), held_as=jnp.bfloat16):
    loudness = shard_levels(own_key, extent, cuts, -0.22, 0.18) if cuts else 1.0
    array = jax.random.normal(own_key, extent, jnp.float32) * scale * loudness
    return jnp.minimum(jnp.maximum(array, -limit), limit).astype(held_as)


def setup_inputs(seed: int = 0, part: int = 0) -> dict:
    arg_keys = jax.random.split(jax.random.key(seed), 7)
    part_keys = jax.random.split(jax.random.fold_in(arg_keys[6], part), 7)
    return {
        "queries": gaussian(part_keys[0], (TOKENS, HEADS * HEAD), 1.0, 6.0, ((0, 8),)),
        "keys": gaussian(part_keys[1], (TOKENS, HEADS * HEAD), 1.0, 6.0, ((0, 8),)),
        "values": gaussian(part_keys[2], (TOKENS, HEADS * HEAD), 1.0, 6.0, ((0, 8),)),
        "doc_starts": draw_doc_starts(jax.random.fold_in(jax.random.fold_in(arg_keys[6], part), 71), part),
        "decay_exps": draw_decay_exps(jax.random.fold_in(arg_keys[6], 71), part),
        "norm_gain": jnp.clip(1.0 + 0.15 * jax.random.normal(arg_keys[5], (HEADS * HEAD,), jnp.float32), 0.25, 1.75),
    }


def lower_rounded(value):
    return lax.optimization_barrier(value.astype(jnp.bfloat16)).astype(jnp.float32)

def block_terms(qpart, key_portion, vpart, starts, decay_rate):
    segment_length = qpart.shape[0]
    count = jnp.cumsum(starts.astype(jnp.int32))
    token_position = jnp.arange(segment_length).astype(jnp.float32)
    same = (count[:, None] == count[None, :]) & (token_position[:, None] >= token_position[None, :])
    gaps = jnp.maximum(token_position[:, None] - token_position[None, :], 0.0)
    weight = jnp.where(same[None], jnp.exp(-decay_rate[:, None, None] * gaps[None]), 0.0)
    qfloat = qpart.astype(jnp.float32)
    key_float_values = key_portion.astype(jnp.float32)
    vfloat = vpart.astype(jnp.float32)
    scores = jnp.einsum('ihd,jhd->hij', qfloat, key_float_values, precision=lax.Precision.HIGHEST)
    weighted = lower_rounded(scores * weight)
    intra = jnp.einsum('hij,jhd->ihd', weighted, vfloat, precision=lax.Precision.HIGHEST)
    fresh = (count == 0).astype(jnp.float32)
    qscale = jnp.exp(-decay_rate[None, :] * (token_position[:, None] + 1.0)) * fresh[:, None]
    trailing_part = (count == count[-1]).astype(jnp.float32)
    key_scale_factor = jnp.exp(-decay_rate[None, :] * (segment_length - 1.0 - token_position[:, None])) * trailing_part[:, None]
    key_decay_factor = lower_rounded(key_float_values * key_scale_factor[:, :, None])
    state = jnp.einsum('jhd,jhe->hde', key_decay_factor, vfloat, precision=lax.Precision.HIGHEST)
    factor = jnp.exp(-decay_rate * segment_length) * (count[-1] == 0).astype(jnp.float32)
    return (intra, qscale, state, factor)

def apply_carry(intra, qpart, qscale, carry):
    cross = jnp.einsum('ihd,hde->ihe', qpart.astype(jnp.float32), lower_rounded(carry), precision=lax.Precision.HIGHEST)
    return intra + qscale[:, :, None] * cross

def head_norm(raw, gain):
    meansq = lax.optimization_barrier(jnp.mean(raw * raw, axis=-1, keepdims=True))
    return (raw * lax.rsqrt(meansq + 1e-06) * gain).astype(jnp.bfloat16)

def reference(queries, keys, values, doc_starts, decay_exps, norm_gain):
    total = queries.shape[0]
    blocks = total // TOK_DEV
    decay_rate = decay_exps.astype(jnp.float32) / 65536.0
    shaped = [a.reshape(blocks, TOK_DEV, HEADS, HEAD) for a in (queries, keys, values)]
    starts = doc_starts.reshape(blocks, TOK_DEV)

    def step(carry, inputs):
        qpart, key_portion, vpart, spart = inputs
        intra, qscale, state, factor = block_terms(qpart, key_portion, vpart, spart, decay_rate)
        out = apply_carry(intra, qpart, qscale, carry)
        return (factor[:, None, None] * carry + state, out)
    start_state = jnp.zeros((HEADS, HEAD, HEAD), jnp.float32)
    final_state, raw = lax.scan(step, start_state, (shaped[0], shaped[1], shaped[2], starts))
    gain = norm_gain.astype(jnp.float32).reshape(HEADS, HEAD)
    result = head_norm(raw, gain)
    return result.reshape(total, HEADS * HEAD)
```

```python
import functools

import jax
import jax.numpy as jnp
from jax import lax
from jax.experimental import pallas as pl
from jax.experimental.pallas import tpu as pltpu
from jax.sharding import PartitionSpec as P

HEADS = 32
HEAD = 128
HALF = HEADS // 2
LAG = 2
F32 = jnp.float32
BF16 = jnp.bfloat16
MESH = pl.DeviceIdType.MESH


def kernel(
    chips, exps, doc, gain, q_hbm, k_hbm, v_hbm, o_ref,
    q, k, v, own, give, got, up_out, up_in, pass_out, pass_in, low, raw, flag_out, flag_in,
    load_sem, give_send, give_recv, up_send, up_recv, pass_send, pass_recv, flag_send, flag_recv,
):
    rows = q.shape[0]
    me = lax.axis_index("ctx")
    core, chip = lax.rem(me, 2), lax.div(me, 2)
    partner, above, below = me + 1 - 2 * core, me + 2, me - 2
    mine, theirs = core * HALF, (1 - core) * HALF

    def load(i, src, dst, first):
        cols = pl.ds(pl.multiple_of(first * HEAD, HALF * HEAD), HALF * HEAD)
        return pltpu.make_async_copy(src.at[:, cols], dst.at[:, cols], load_sem.at[i])

    loads = [
        load(0, k_hbm, k, theirs), load(1, v_hbm, v, theirs), load(2, k_hbm, k, mine),
        load(3, v_hbm, v, mine), load(4, q_hbm, q, mine), load(5, q_hbm, q, theirs),
    ]
    for c in loads:
        c.start()

    barrier = pltpu.get_barrier_semaphore()
    pl.semaphore_signal(barrier, inc=1, device_id={"ctx": partner}, device_id_type=MESH)

    @pl.when(chip > 0)
    def _():
        pl.semaphore_signal(barrier, inc=1, device_id={"ctx": below}, device_id_type=MESH)

    starts = doc[...].astype(F32)
    sub = lax.broadcasted_iota(jnp.int32, (rows, rows), 0)
    lane = lax.broadcasted_iota(jnp.int32, (rows, rows), 1)
    wide = jnp.broadcast_to(starts, (rows, rows))
    count_col = jnp.sum(jnp.where(lane <= sub, wide, 0.0), axis=1, keepdims=True)
    start_col = jnp.sum(jnp.where(lane == sub, wide, 0.0), axis=1, keepdims=True)
    count_row = jnp.sum(jnp.where(sub <= lane, jnp.broadcast_to(start_col, (rows, rows)), 0.0), axis=0, keepdims=True)
    total = jnp.sum(starts, axis=1, keepdims=True)
    same = (count_col == count_row) & (sub >= lane)
    gaps = jnp.maximum(sub - lane, 0).astype(F32)
    place = lax.broadcasted_iota(jnp.int32, (rows, HEAD), 0).astype(F32)
    fresh = jnp.broadcast_to(jnp.where(count_col == 0.0, 1.0, 0.0), (rows, HEAD))
    trail = jnp.broadcast_to(jnp.where(count_col == total, 1.0, 0.0), (rows, HEAD))
    whole = jnp.where(total == 0.0, 1.0, 0.0)
    flag_out[...] = jnp.broadcast_to(whole, flag_out.shape)

    def columns(h):
        return pl.ds(pl.multiple_of(h * HEAD, HEAD), HEAD)

    def rate_of(h):
        return exps[h].astype(F32) * (1.0 / 65536.0)

    def state(h):
        scale = jnp.exp(-rate_of(h) * (rows - 1.0 - place)) * trail
        kd = (k[:, columns(h)].astype(F32) * scale).astype(BF16)
        return lax.dot_general(kd, v[:, columns(h)], (((0,), (0,)), ((), ())), preferred_element_type=F32)

    def remote(src, dst, ssem, rsem, dev):
        return pltpu.make_async_remote_copy(
            src_ref=src, dst_ref=dst, send_sem=ssem, recv_sem=rsem, device_id={"ctx": dev}, device_id_type=MESH
        )

    def give_copy(g):
        return remote(give.at[g], got.at[g], give_send.at[g], give_recv.at[g], partner)

    def up_copy(g):
        return remote(up_out.at[g], up_in.at[g], up_send.at[g], up_recv.at[g], above)

    def pass_copy(g):
        return remote(pass_out.at[g], pass_in.at[g], pass_send.at[g], pass_recv.at[g], partner)

    flag_copy = remote(flag_out, flag_in, flag_send.at[0], flag_recv.at[0], partner)

    def chain(g, first):
        give_copy(g).wait_recv()
        held, other = own[g], got[g].astype(F32)
        at0 = core == 0
        s0, s1 = jnp.where(at0, held, other), jnp.where(at0, other, held)
        full = jnp.exp(jnp.full((1, HEAD), -rate_of(mine + g) * rows, F32))
        f_me, f_partner = full * flag_out[0:1, :], full * flag_in[0:1, :]
        f0, f1 = jnp.where(at0, f_me, f_partner), jnp.where(at0, f_partner, f_me)
        if first:
            before = jnp.zeros((HEAD, HEAD), F32)
            middle = s0
        else:
            up_copy(g).wait_recv()
            before = up_in[g].astype(F32)
            middle = f0 * before + s0

        @pl.when(chip < chips - 1)
        def _():
            up_out[g] = (f1 * middle + s1).astype(BF16)
            up_copy(g).start()

        pass_out[g] = jnp.where(at0, middle, before).astype(BF16)
        pass_copy(g).start()
        low[g] = jnp.where(at0, before, middle).astype(BF16)

    def intra(h):
        cols = columns(h)
        scores = lax.dot_general(q[:, cols], k[:, cols], (((1,), (1,)), ((), ())), preferred_element_type=F32)
        weight = jnp.where(same, jnp.exp(-rate_of(h) * gaps), 0.0)
        raw[:, cols] = jnp.dot((scores * weight).astype(BF16), v[:, cols], preferred_element_type=F32)

    def output(h, carry):
        cols = columns(h)
        qscale = jnp.exp(-rate_of(h) * (place + 1.0)) * fresh
        r = raw[:, cols] + qscale * jnp.dot(q[:, cols], carry, preferred_element_type=F32)
        meansq = jnp.mean(r * r, axis=-1, keepdims=True)
        o_ref[:, cols] = (r * lax.rsqrt(meansq + 1e-06) * gain[pl.ds(h, 1), :]).astype(BF16)

    loads[0].wait()
    loads[1].wait()
    pl.semaphore_wait(barrier, jnp.where(chip < chips - 1, 2, 1))
    flag_copy.start()
    loads[2].wait()
    loads[3].wait()

    def step_a(g, _):
        @pl.when(g < HALF)
        def _():
            give[g] = state(theirs + g).astype(BF16)
            give_copy(g).start()
            own[g] = state(mine + g)

        @pl.when(g == LAG)
        def _():
            flag_copy.wait_recv()

        @pl.when((g >= LAG) & (chip == 0))
        def _():
            chain(g - LAG, True)

        return 0

    lax.fori_loop(0, HALF + LAG, step_a, 0)
    loads[4].wait()
    loads[5].wait()

    def both(g):
        intra(mine + g)
        intra(theirs + g)

    @pl.when(chip >= 2)
    def _():
        lax.fori_loop(0, HALF, lambda g, _: (both(g), 0)[1], 0)

    def step_c(g, _):
        @pl.when((g < HALF) & (chip > 0))
        def _():
            chain(g, False)

        @pl.when((g < HALF) & (chip < 2))
        def _():
            both(g)

        @pl.when(g >= LAG)
        def _():
            e = g - LAG
            output(mine + e, low[e])
            pass_copy(e).wait_recv()
            output(theirs + e, pass_in[e])

        return 0

    lax.fori_loop(0, HALF + LAG, step_c, 0)

    flag_copy.wait_send()

    def drain(g, _):
        give_copy(g).wait_send()
        pass_copy(g).wait_send()

        @pl.when(chip < chips - 1)
        def _():
            up_copy(g).wait_send()

        return 0

    lax.fori_loop(0, HALF, drain, 0)


def on_device(queries, keys, values, doc_starts, decay_exps, norm_gain):
    rows = queries.shape[0]
    chips = lax.axis_size("ctx") // 2
    vmem, smem, anywhere = (pl.BlockSpec(memory_space=m) for m in (pltpu.VMEM, pltpu.SMEM, pl.ANY))
    half = (HALF, HEAD, HEAD)
    sem = pltpu.SemaphoreType.DMA
    return pl.pallas_call(
        functools.partial(kernel, chips),
        out_shape=jax.ShapeDtypeStruct(queries.shape, BF16),
        in_specs=[smem, vmem, vmem, anywhere, anywhere, anywhere],
        out_specs=vmem,
        scratch_shapes=[
            *[pltpu.VMEM(queries.shape, BF16)] * 3,
            pltpu.VMEM(half, F32),
            *[pltpu.VMEM(half, BF16)] * 7,
            pltpu.VMEM(queries.shape, F32),
            pltpu.VMEM((8, HEAD), F32),
            pltpu.VMEM((8, HEAD), F32),
            sem((6,)),
            *[sem((HALF,))] * 6,
            sem((1,)),
            sem((1,)),
        ],
        compiler_params=pltpu.CompilerParams(
            collective_id=0, has_side_effects=True, vmem_limit_bytes=32 * 2**20
        ),
        name="chain",
    )(
        decay_exps,
        doc_starts.reshape(1, rows),
        norm_gain.reshape(HEADS, HEAD),
        queries, keys, values,
    )


def solution(mesh):
    return jax.shard_map(
        on_device,
        mesh=mesh,
        in_specs=(
            P(("dp", "ctx"), None),
            P(("dp", "ctx"), None),
            P(("dp", "ctx"), None),
            P(("dp", "ctx")),
            P(),
            P(),
        ),
        out_specs=P(("dp", "ctx"), None),
        check_vma=False,
    )
```

```python
import functools

import jax
import jax.numpy as jnp
from jax import lax
from jax.experimental import pallas as pl
from jax.experimental.pallas import tpu as pltpu
from jax.sharding import PartitionSpec as P

HEADS = 32
HEAD = 128
HALF = HEADS // 2
UNROLL = 2
STEPS = HALF // UNROLL
F32 = jnp.float32
BF16 = jnp.bfloat16
MESH = pl.DeviceIdType.MESH


def kernel(
    chips, exps_hbm, doc_hbm, gain_hbm, q_hbm, k_hbm, v_hbm, o_ref,
    exps, doc, gain, q, k, v, own, give, got, up_out, up_in, pass_out, pass_in, low, raw, flag_out, flag_in,
    load_sem, give_send, give_recv, up_send, up_recv, pass_send, pass_recv, flag_send, flag_recv,
):
    rows = q.shape[0]
    me = lax.axis_index("ctx")
    core, chip = lax.rem(me, 2), lax.div(me, 2)
    partner, above, below = me + 1 - 2 * core, me + 2, me - 2
    mine, theirs = core * HALF, (1 - core) * HALF

    def load(i, src, dst, first):
        cols = pl.ds(pl.multiple_of(first * HEAD, HALF * HEAD), HALF * HEAD)
        return pltpu.make_async_copy(src.at[:, cols], dst.at[:, cols], load_sem.at[i])

    loads = [
        load(0, k_hbm, k, theirs), load(1, v_hbm, v, theirs), load(2, k_hbm, k, mine),
        load(3, v_hbm, v, mine), load(4, q_hbm, q, mine), load(5, q_hbm, q, theirs),
    ]
    small = [
        pltpu.make_async_copy(src, dst, load_sem.at[6 + i])
        for i, (src, dst) in enumerate(((doc_hbm, doc), (exps_hbm, exps), (gain_hbm, gain)))
    ]
    for c in small + loads:
        c.start()

    barrier = pltpu.get_barrier_semaphore()
    pl.semaphore_signal(barrier, inc=1, device_id={"ctx": partner}, device_id_type=MESH)

    @pl.when(chip > 0)
    def _():
        pl.semaphore_signal(barrier, inc=1, device_id={"ctx": below}, device_id_type=MESH)

    for c in small:
        c.wait()
    starts = doc[...].astype(F32)
    sub = lax.broadcasted_iota(jnp.int32, (rows, rows), 0)
    lane = lax.broadcasted_iota(jnp.int32, (rows, rows), 1)
    wide = jnp.broadcast_to(starts, (rows, rows))
    count_col = jnp.sum(jnp.where(lane <= sub, wide, 0.0), axis=1, keepdims=True)
    start_col = jnp.sum(jnp.where(lane == sub, wide, 0.0), axis=1, keepdims=True)
    count_row = jnp.sum(jnp.where(sub <= lane, jnp.broadcast_to(start_col, (rows, rows)), 0.0), axis=0, keepdims=True)
    total = jnp.sum(starts, axis=1, keepdims=True)
    same = (count_col == count_row) & (sub >= lane)
    gaps = jnp.maximum(sub - lane, 0).astype(F32)
    place = lax.broadcasted_iota(jnp.int32, (rows, HEAD), 0).astype(F32)
    fresh = jnp.broadcast_to(jnp.where(count_col == 0.0, 1.0, 0.0), (rows, HEAD))
    trail = jnp.broadcast_to(jnp.where(count_col == total, 1.0, 0.0), (rows, HEAD))
    whole = jnp.where(total == 0.0, 1.0, 0.0)
    flag_out[...] = jnp.broadcast_to(whole, flag_out.shape)

    def columns(h):
        return pl.ds(pl.multiple_of(h * HEAD, HEAD), HEAD)

    def rate_of(h):
        return exps[h].astype(F32) * (1.0 / 65536.0)

    def state(h):
        scale = jnp.exp(-rate_of(h) * (rows - 1.0 - place)) * trail
        kd = (k[:, columns(h)].astype(F32) * scale).astype(BF16)
        return lax.dot_general(kd, v[:, columns(h)], (((0,), (0,)), ((), ())), preferred_element_type=F32)

    def remote(src, dst, ssem, rsem, dev):
        return pltpu.make_async_remote_copy(
            src_ref=src, dst_ref=dst, send_sem=ssem, recv_sem=rsem, device_id={"ctx": dev}, device_id_type=MESH
        )

    def give_copy(g):
        return remote(give.at[g], got.at[g], give_send.at[g], give_recv.at[g], partner)

    def up_copy(g):
        return remote(up_out.at[g], up_in.at[g], up_send.at[g], up_recv.at[g], above)

    def pass_copy(g):
        return remote(pass_out.at[g], pass_in.at[g], pass_send.at[g], pass_recv.at[g], partner)

    flag_copy = remote(flag_out, flag_in, flag_send.at[0], flag_recv.at[0], partner)

    def chain(step, first):
        at0 = core == 0
        heads = [step * UNROLL + u for u in range(UNROLL)]
        for g in heads:
            give_copy(g).wait_recv()
            if not first:
                up_copy(g).wait_recv()
        ups, passes, lows = [], [], []
        for g in heads:
            held, other = own[g], got[g].astype(F32)
            s0, s1 = jnp.where(at0, held, other), jnp.where(at0, other, held)
            full = jnp.exp(jnp.full((1, HEAD), -rate_of(mine + g) * rows, F32))
            f_me, f_partner = full * flag_out[0:1, :], full * flag_in[0:1, :]
            f0, f1 = jnp.where(at0, f_me, f_partner), jnp.where(at0, f_partner, f_me)
            if first:
                before = jnp.zeros((HEAD, HEAD), F32)
                middle = s0
            else:
                before = up_in[g].astype(F32)
                middle = f0 * before + s0
            ups.append((f1 * middle + s1).astype(BF16))
            passes.append(jnp.where(at0, middle, before).astype(BF16))
            lows.append(jnp.where(at0, before, middle).astype(BF16))
        for g, a, b, c in zip(heads, ups, passes, lows):
            up_out[g], pass_out[g], low[g] = a, b, c

        @pl.when(chip < chips - 1)
        def _():
            for g in heads:
                up_copy(g).start()

        for g in heads:
            pass_copy(g).start()

    def pairs(step):
        return [step * UNROLL + u for u in range(UNROLL)]

    def both(step):
        heads = [first + g for first in (mine, theirs) for g in pairs(step)]
        scores = [
            lax.dot_general(q[:, columns(h)], k[:, columns(h)], (((1,), (1,)), ((), ())), preferred_element_type=F32)
            for h in heads
        ]
        weighted = [
            (x * jnp.where(same, jnp.exp(-rate_of(h) * gaps), 0.0)).astype(BF16) for x, h in zip(scores, heads)
        ]
        sums = [jnp.dot(w, v[:, columns(h)], preferred_element_type=F32) for w, h in zip(weighted, heads)]
        for x, h in zip(sums, heads):
            raw[:, columns(h)] = x

    def output(step):
        for g in pairs(step):
            pass_copy(g).wait_recv()
        heads = [first + g for first in (mine, theirs) for g in pairs(step)]
        carries = [ref[g] for ref in (low, pass_in) for g in pairs(step)]
        cross = [jnp.dot(q[:, columns(h)], c, preferred_element_type=F32) for h, c in zip(heads, carries)]
        raws = [
            raw[:, columns(h)] + jnp.exp(-rate_of(h) * (place + 1.0)) * fresh * x for h, x in zip(heads, cross)
        ]
        means = [jnp.mean(r * r, axis=-1, keepdims=True) for r in raws]
        outs = [
            (r * lax.rsqrt(m + 1e-06) * gain[pl.ds(h, 1), :]).astype(BF16) for r, m, h in zip(raws, means, heads)
        ]
        for x, h in zip(outs, heads):
            o_ref[:, columns(h)] = x

    loads[0].wait()
    loads[1].wait()
    pl.semaphore_wait(barrier, jnp.where(chip < chips - 1, 2, 1))
    flag_copy.start()
    loads[2].wait()
    loads[3].wait()

    def step_a(step, _):
        @pl.when(step < STEPS)
        def _():
            give_now = [state(theirs + g).astype(BF16) for g in pairs(step)]
            own_now = [state(mine + g) for g in pairs(step)]
            for g, a, b in zip(pairs(step), give_now, own_now):
                give[g], own[g] = a, b
            for g in pairs(step):
                give_copy(g).start()

        @pl.when(step == 1)
        def _():
            flag_copy.wait_recv()

        @pl.when((step >= 1) & (chip == 0))
        def _():
            chain(step - 1, True)

        return 0

    lax.fori_loop(0, STEPS + 1, step_a, 0)
    loads[4].wait()
    loads[5].wait()

    @pl.when(chip >= 2)
    def _():
        lax.fori_loop(0, STEPS, lambda step, _: (both(step), 0)[1], 0)

    def step_c(step, _):
        @pl.when((step < STEPS) & (chip > 0))
        def _():
            chain(step, False)

        @pl.when((step < STEPS) & (chip < 2))
        def _():
            both(step)

        @pl.when(step >= 1)
        def _():
            output(step - 1)

        return 0

    lax.fori_loop(0, STEPS + 1, step_c, 0)

    flag_copy.wait_send()

    def drain(g, _):
        give_copy(g).wait_send()
        pass_copy(g).wait_send()

        @pl.when(chip < chips - 1)
        def _():
            up_copy(g).wait_send()

        return 0

    lax.fori_loop(0, HALF, drain, 0)


def on_device(queries, keys, values, doc_starts, decay_exps, norm_gain):
    rows = queries.shape[0]
    chips = lax.axis_size("ctx") // 2
    vmem, hbm = (pl.BlockSpec(memory_space=m) for m in (pltpu.VMEM, pltpu.HBM))
    half = (HALF, HEAD, HEAD)
    sem = pltpu.SemaphoreType.DMA
    return pl.pallas_call(
        functools.partial(kernel, chips),
        out_shape=jax.ShapeDtypeStruct(queries.shape, BF16),
        in_specs=[hbm] * 6,
        out_specs=vmem,
        scratch_shapes=[
            pltpu.SMEM((HEADS,), jnp.int32),
            pltpu.VMEM((1, rows), jnp.int32),
            pltpu.VMEM((HEADS, HEAD), F32),
            *[pltpu.VMEM(queries.shape, BF16)] * 3,
            pltpu.VMEM(half, F32),
            *[pltpu.VMEM(half, BF16)] * 7,
            pltpu.VMEM(queries.shape, F32),
            pltpu.VMEM((8, HEAD), F32),
            pltpu.VMEM((8, HEAD), F32),
            sem((9,)),
            *[sem((HALF,))] * 6,
            sem((1,)),
            sem((1,)),
        ],
        compiler_params=pltpu.CompilerParams(
            collective_id=0, has_side_effects=True, vmem_limit_bytes=60 * 2**20
        ),
        name="chain",
    )(
        decay_exps,
        doc_starts.reshape(1, rows),
        norm_gain.reshape(HEADS, HEAD),
        queries, keys, values,
    )


def solution(mesh):
    return jax.shard_map(
        on_device,
        mesh=mesh,
        in_specs=(
            P(("dp", "ctx"), None),
            P(("dp", "ctx"), None),
            P(("dp", "ctx"), None),
            P(("dp", "ctx")),
            P(),
            P(),
        ),
        out_specs=P(("dp", "ctx"), None),
        check_vma=False,
    )
```

```python
import functools

import jax
import jax.numpy as jnp
from jax import lax
from jax.experimental import pallas as pl
from jax.experimental.pallas import tpu as pltpu
from jax.sharding import PartitionSpec as P

HEADS = 32
HEAD = 128
HALF = HEADS // 2
UNROLL = 2
STEPS = HALF // UNROLL
PIECES = 2
PIECE = HEAD // PIECES
F32 = jnp.float32
BF16 = jnp.bfloat16
MESH = pl.DeviceIdType.MESH


def kernel(
    chips, exps_hbm, doc_hbm, gain_hbm, q_hbm, k_hbm, v_hbm, o_ref,
    exps, doc, gain, q, k, v, own, give, got, up_out, up_in, pass_out, pass_in, low, raw, flag_out, flag_in,
    load_sem, give_send, give_recv, up_send, up_recv, pass_send, pass_recv, flag_send, flag_recv,
):
    rows = q.shape[0]
    me = lax.axis_index("ctx")
    core, chip = lax.rem(me, 2), lax.div(me, 2)
    partner, above, below = me + 1 - 2 * core, me + 2, me - 2
    mine, theirs = core * HALF, (1 - core) * HALF

    def load(i, src, dst, first):
        cols = pl.ds(pl.multiple_of(first * HEAD, HALF * HEAD), HALF * HEAD)
        return pltpu.make_async_copy(src.at[:, cols], dst.at[:, cols], load_sem.at[i])

    loads = [
        load(0, k_hbm, k, theirs), load(1, v_hbm, v, theirs), load(2, k_hbm, k, mine),
        load(3, v_hbm, v, mine), load(4, q_hbm, q, mine), load(5, q_hbm, q, theirs),
    ]
    small = [
        pltpu.make_async_copy(src, dst, load_sem.at[6 + i])
        for i, (src, dst) in enumerate(((doc_hbm, doc), (exps_hbm, exps), (gain_hbm, gain)))
    ]
    for c in small + loads:
        c.start()

    barrier = pltpu.get_barrier_semaphore()
    pl.semaphore_signal(barrier, inc=1, device_id={"ctx": partner}, device_id_type=MESH)

    @pl.when(chip > 0)
    def _():
        pl.semaphore_signal(barrier, inc=1, device_id={"ctx": below}, device_id_type=MESH)

    for c in small:
        c.wait()
    starts = doc[...].astype(F32)
    sub = lax.broadcasted_iota(jnp.int32, (rows, rows), 0)
    lane = lax.broadcasted_iota(jnp.int32, (rows, rows), 1)
    wide = jnp.broadcast_to(starts, (rows, rows))
    count_col = jnp.sum(jnp.where(lane <= sub, wide, 0.0), axis=1, keepdims=True)
    start_col = jnp.sum(jnp.where(lane == sub, wide, 0.0), axis=1, keepdims=True)
    count_row = jnp.sum(jnp.where(sub <= lane, jnp.broadcast_to(start_col, (rows, rows)), 0.0), axis=0, keepdims=True)
    total = jnp.sum(starts, axis=1, keepdims=True)
    same = (count_col == count_row) & (sub >= lane)
    gaps = jnp.maximum(sub - lane, 0).astype(F32)
    place = lax.broadcasted_iota(jnp.int32, (rows, HEAD), 0).astype(F32)
    fresh = jnp.broadcast_to(jnp.where(count_col == 0.0, 1.0, 0.0), (rows, HEAD))
    trail = jnp.broadcast_to(jnp.where(count_col == total, 1.0, 0.0), (rows, HEAD))
    whole = jnp.where(total == 0.0, 1.0, 0.0)
    flag_out[...] = jnp.broadcast_to(whole, flag_out.shape)

    def columns(h):
        return pl.ds(pl.multiple_of(h * HEAD, HEAD), HEAD)

    def rate_of(h):
        return exps[h].astype(F32) * (1.0 / 65536.0)

    def state(h):
        scale = jnp.exp(-rate_of(h) * (rows - 1.0 - place)) * trail
        kd = (k[:, columns(h)].astype(F32) * scale).astype(BF16)
        return lax.dot_general(kd, v[:, columns(h)], (((0,), (0,)), ((), ())), preferred_element_type=F32)

    def remote(src, dst, ssem, rsem, dev):
        return pltpu.make_async_remote_copy(
            src_ref=src, dst_ref=dst, send_sem=ssem, recv_sem=rsem, device_id={"ctx": dev}, device_id_type=MESH
        )

    def give_copy(g):
        return remote(give.at[g], got.at[g], give_send.at[g], give_recv.at[g], partner)

    def up_copy(g, p):
        part = (g, pl.ds(p * PIECE, PIECE))
        i = g * PIECES + p
        return remote(up_out.at[part], up_in.at[part], up_send.at[i], up_recv.at[i], above)

    def pass_copy(g):
        return remote(pass_out.at[g], pass_in.at[g], pass_send.at[g], pass_recv.at[g], partner)

    flag_copy = remote(flag_out, flag_in, flag_send.at[0], flag_recv.at[0], partner)

    def chain(step, first):
        at0 = core == 0
        for u in range(UNROLL):
            g = step * UNROLL + u
            give_copy(g).wait_recv()
            full = jnp.exp(jnp.full((1, HEAD), -rate_of(mine + g) * rows, F32))
            f_me, f_partner = full * flag_out[0:1, :], full * flag_in[0:1, :]
            f0, f1 = jnp.where(at0, f_me, f_partner), jnp.where(at0, f_partner, f_me)
            for p in range(PIECES):
                part = (g, pl.ds(p * PIECE, PIECE))
                held, other = own[part], got[part].astype(F32)
                s0, s1 = jnp.where(at0, held, other), jnp.where(at0, other, held)
                if first:
                    before = jnp.zeros((PIECE, HEAD), F32)
                    middle = s0
                else:
                    up_copy(g, p).wait_recv()
                    before = up_in[part].astype(F32)
                    middle = f0 * before + s0
                up_out[part] = (f1 * middle + s1).astype(BF16)

                @pl.when(chip < chips - 1)
                def _():
                    up_copy(g, p).start()

                pass_out[part] = jnp.where(at0, middle, before).astype(BF16)
                low[part] = jnp.where(at0, before, middle).astype(BF16)
            pass_copy(g).start()

    def pairs(step):
        return [step * UNROLL + u for u in range(UNROLL)]

    def both(step):
        heads = [first + g for first in (mine, theirs) for g in pairs(step)]
        scores = [
            lax.dot_general(q[:, columns(h)], k[:, columns(h)], (((1,), (1,)), ((), ())), preferred_element_type=F32)
            for h in heads
        ]
        weighted = [
            (x * jnp.where(same, jnp.exp(-rate_of(h) * gaps), 0.0)).astype(BF16) for x, h in zip(scores, heads)
        ]
        sums = [jnp.dot(w, v[:, columns(h)], preferred_element_type=F32) for w, h in zip(weighted, heads)]
        for x, h in zip(sums, heads):
            raw[:, columns(h)] = x

    def output(step):
        for first, ref in ((mine, low), (theirs, pass_in)):
            heads = [first + g for g in pairs(step)]
            if ref is pass_in:
                for g in pairs(step):
                    pass_copy(g).wait_recv()
            carries = [ref[g] for g in pairs(step)]
            cross = [jnp.dot(q[:, columns(h)], c, preferred_element_type=F32) for h, c in zip(heads, carries)]
            raws = [
                raw[:, columns(h)] + jnp.exp(-rate_of(h) * (place + 1.0)) * fresh * x for h, x in zip(heads, cross)
            ]
            means = [jnp.mean(r * r, axis=-1, keepdims=True) for r in raws]
            outs = [
                (r * lax.rsqrt(m + 1e-06) * gain[pl.ds(h, 1), :]).astype(BF16) for r, m, h in zip(raws, means, heads)
            ]
            for x, h in zip(outs, heads):
                o_ref[:, columns(h)] = x

    loads[0].wait()
    loads[1].wait()
    pl.semaphore_wait(barrier, jnp.where(chip < chips - 1, 2, 1))
    flag_copy.start()
    loads[2].wait()
    loads[3].wait()

    def step_a(step, _):
        @pl.when(step < STEPS)
        def _():
            give_now = [state(theirs + g).astype(BF16) for g in pairs(step)]
            for g, a in zip(pairs(step), give_now):
                give[g] = a
            for g in pairs(step):
                give_copy(g).start()
            own_now = [state(mine + g) for g in pairs(step)]
            for g, b in zip(pairs(step), own_now):
                own[g] = b

        @pl.when(step == 1)
        def _():
            flag_copy.wait_recv()

        @pl.when((step >= 1) & (chip == 0))
        def _():
            chain(step - 1, True)

        return 0

    lax.fori_loop(0, STEPS + 1, step_a, 0)
    loads[4].wait()
    loads[5].wait()

    @pl.when(chip >= 2)
    def _():
        lax.fori_loop(0, STEPS, lambda step, _: (both(step), 0)[1], 0)

    def step_c(step, _):
        @pl.when((step < STEPS) & (chip > 0))
        def _():
            chain(step, False)

        @pl.when((step < STEPS) & (chip < 2))
        def _():
            both(step)

        @pl.when(step >= 1)
        def _():
            output(step - 1)

        return 0

    lax.fori_loop(0, STEPS + 1, step_c, 0)

    flag_copy.wait_send()

    def drain(g, _):
        give_copy(g).wait_send()
        pass_copy(g).wait_send()

        @pl.when(chip < chips - 1)
        def _():
            for p in range(PIECES):
                up_copy(g, p).wait_send()

        return 0

    lax.fori_loop(0, HALF, drain, 0)


def on_device(queries, keys, values, doc_starts, decay_exps, norm_gain):
    rows = queries.shape[0]
    chips = lax.axis_size("ctx") // 2
    vmem, hbm = (pl.BlockSpec(memory_space=m) for m in (pltpu.VMEM, pltpu.HBM))
    half = (HALF, HEAD, HEAD)
    sem = pltpu.SemaphoreType.DMA
    return pl.pallas_call(
        functools.partial(kernel, chips),
        out_shape=jax.ShapeDtypeStruct(queries.shape, BF16),
        in_specs=[hbm] * 6,
        out_specs=vmem,
        scratch_shapes=[
            pltpu.SMEM((HEADS,), jnp.int32),
            pltpu.VMEM((1, rows), jnp.int32),
            pltpu.VMEM((HEADS, HEAD), F32),
            *[pltpu.VMEM(queries.shape, BF16)] * 3,
            pltpu.VMEM(half, F32),
            *[pltpu.VMEM(half, BF16)] * 7,
            pltpu.VMEM(queries.shape, F32),
            pltpu.VMEM((8, HEAD), F32),
            pltpu.VMEM((8, HEAD), F32),
            sem((9,)),
            *[sem((HALF,))] * 2,
            *[sem((HALF * PIECES,))] * 2,
            *[sem((HALF,))] * 2,
            sem((1,)),
            sem((1,)),
        ],
        compiler_params=pltpu.CompilerParams(
            collective_id=0, has_side_effects=True, vmem_limit_bytes=32 * 2**20
        ),
        name="chain",
    )(
        *[
            pltpu.with_memory_space_constraint(a, pltpu.HBM)
            for a in (
                decay_exps,
                doc_starts.reshape(1, rows),
                norm_gain.reshape(HEADS, HEAD),
                queries, keys, values,
            )
        ]
    )


def solution(mesh):
    return jax.shard_map(
        on_device,
        mesh=mesh,
        in_specs=(
            P(("dp", "ctx"), None),
            P(("dp", "ctx"), None),
            P(("dp", "ctx"), None),
            P(("dp", "ctx")),
            P(),
            P(),
        ),
        out_specs=P(("dp", "ctx"), None),
        check_vma=False,
    )
```

```python
import functools

import jax
import jax.numpy as jnp
from jax import lax
from jax.experimental import pallas as pl
from jax.experimental.pallas import tpu as pltpu
from jax.sharding import PartitionSpec as P

HEADS = 32
HEAD = 128
HALF = HEADS // 2
UNROLL = 2
STEPS = HALF // UNROLL
PIECES = 2
PIECE = HEAD // PIECES
F32 = jnp.float32
BF16 = jnp.bfloat16
MESH = pl.DeviceIdType.MESH


def kernel(
    chips, exps_hbm, doc_hbm, gain_hbm, q_hbm, k_hbm, v_hbm, o_ref,
    exps, doc, gain, q, k, v, own, give, got, up_out, up_in, pass_out, pass_in, low, raw, flag_out, flag_in,
    load_sem, give_send, give_recv, up_send, up_recv, pass_send, pass_recv, flag_send, flag_recv,
):
    rows = q.shape[0]
    me = lax.axis_index("ctx")
    core, chip = lax.rem(me, 2), lax.div(me, 2)
    partner, above, below = me + 1 - 2 * core, me + 2, me - 2
    mine, theirs = core * HALF, (1 - core) * HALF

    def load(i, src, dst, first):
        cols = pl.ds(pl.multiple_of(first * HEAD, HALF * HEAD), HALF * HEAD)
        return pltpu.make_async_copy(src.at[:, cols], dst.at[:, cols], load_sem.at[i])

    loads = [
        load(0, k_hbm, k, theirs), load(1, v_hbm, v, theirs), load(2, k_hbm, k, mine),
        load(3, v_hbm, v, mine), load(4, q_hbm, q, mine), load(5, q_hbm, q, theirs),
    ]
    small = [
        pltpu.make_async_copy(src, dst, load_sem.at[6 + i])
        for i, (src, dst) in enumerate(((doc_hbm, doc), (exps_hbm, exps), (gain_hbm, gain)))
    ]
    for c in small + loads:
        c.start()

    barrier = pltpu.get_barrier_semaphore()
    pl.semaphore_signal(barrier, inc=1, device_id={"ctx": partner}, device_id_type=MESH)

    @pl.when(chip > 0)
    def _():
        pl.semaphore_signal(barrier, inc=1, device_id={"ctx": below}, device_id_type=MESH)

    for c in small:
        c.wait()
    starts = doc[...].astype(F32)
    sub = lax.broadcasted_iota(jnp.int32, (rows, rows), 0)
    lane = lax.broadcasted_iota(jnp.int32, (rows, rows), 1)
    wide = jnp.broadcast_to(starts, (rows, rows))
    count_col = jnp.sum(jnp.where(lane <= sub, wide, 0.0), axis=1, keepdims=True)
    start_col = jnp.sum(jnp.where(lane == sub, wide, 0.0), axis=1, keepdims=True)
    count_row = jnp.sum(jnp.where(sub <= lane, jnp.broadcast_to(start_col, (rows, rows)), 0.0), axis=0, keepdims=True)
    total = jnp.sum(starts, axis=1, keepdims=True)
    same = (count_col == count_row) & (sub >= lane)
    gaps = jnp.maximum(sub - lane, 0).astype(F32)
    place = lax.broadcasted_iota(jnp.int32, (rows, HEAD), 0).astype(F32)
    fresh = jnp.broadcast_to(jnp.where(count_col == 0.0, 1.0, 0.0), (rows, HEAD))
    trail = jnp.broadcast_to(jnp.where(count_col == total, 1.0, 0.0), (rows, HEAD))
    whole = jnp.where(total == 0.0, 1.0, 0.0)
    flag_out[...] = jnp.broadcast_to(whole, flag_out.shape)

    def columns(h):
        return pl.ds(pl.multiple_of(h * HEAD, HEAD), HEAD)

    def rate_of(h):
        return exps[h].astype(F32) * (1.0 / 65536.0)

    def state(h):
        scale = jnp.exp(-rate_of(h) * (rows - 1.0 - place)) * trail
        kd = (k[:, columns(h)].astype(F32) * scale).astype(BF16)
        return lax.dot_general(kd, v[:, columns(h)], (((0,), (0,)), ((), ())), preferred_element_type=F32)

    def remote(src, dst, ssem, rsem, dev):
        return pltpu.make_async_remote_copy(
            src_ref=src, dst_ref=dst, send_sem=ssem, recv_sem=rsem, device_id={"ctx": dev}, device_id_type=MESH
        )

    def give_copy(g):
        return remote(give.at[g], got.at[g], give_send.at[g], give_recv.at[g], partner)

    def up_copy(g, p):
        part = (g, pl.ds(p * PIECE, PIECE))
        i = g * PIECES + p
        return remote(up_out.at[part], up_in.at[part], up_send.at[i], up_recv.at[i], above)

    def pass_copy(g):
        return remote(pass_out.at[g], pass_in.at[g], pass_send.at[g], pass_recv.at[g], partner)

    flag_copy = remote(flag_out, flag_in, flag_send.at[0], flag_recv.at[0], partner)

    def chain(step, first):
        at0 = core == 0
        for u in range(UNROLL):
            g = step * UNROLL + u
            give_copy(g).wait_recv()
            full = jnp.exp(jnp.full((1, HEAD), -rate_of(mine + g) * rows, F32))
            f_me, f_partner = full * flag_out[0:1, :], full * flag_in[0:1, :]
            f0, f1 = jnp.where(at0, f_me, f_partner), jnp.where(at0, f_partner, f_me)
            for p in range(PIECES):
                part = (g, pl.ds(p * PIECE, PIECE))
                held, other = own[part], got[part].astype(F32)
                s0, s1 = jnp.where(at0, held, other), jnp.where(at0, other, held)
                if first:
                    before = jnp.zeros((PIECE, HEAD), F32)
                    middle = s0
                else:
                    up_copy(g, p).wait_recv()
                    before = up_in[part].astype(F32)
                    middle = f0 * before + s0
                up_out[part] = (f1 * middle + s1).astype(BF16)

                @pl.when(chip < chips - 1)
                def _():
                    up_copy(g, p).start()

                pass_out[part] = jnp.where(at0, middle, before).astype(BF16)
                low[part] = jnp.where(at0, before, middle).astype(BF16)
            pass_copy(g).start()

    def pairs(step):
        return [step * UNROLL + u for u in range(UNROLL)]

    def both(step):
        heads = [first + g for first in (mine, theirs) for g in pairs(step)]
        scores = [
            lax.dot_general(q[:, columns(h)], k[:, columns(h)], (((1,), (1,)), ((), ())), preferred_element_type=F32)
            for h in heads
        ]
        weighted = [
            (x * jnp.where(same, jnp.exp(-rate_of(h) * gaps), 0.0)).astype(BF16) for x, h in zip(scores, heads)
        ]
        sums = [jnp.dot(w, v[:, columns(h)], preferred_element_type=F32) for w, h in zip(weighted, heads)]
        for x, h in zip(sums, heads):
            raw[:, columns(h)] = x

    def output(step):
        for first, ref in ((mine, low), (theirs, pass_in)):
            heads = [first + g for g in pairs(step)]
            if ref is pass_in:
                for g in pairs(step):
                    pass_copy(g).wait_recv()
            carries = [ref[g] for g in pairs(step)]
            cross = [jnp.dot(q[:, columns(h)], c, preferred_element_type=F32) for h, c in zip(heads, carries)]
            raws = [
                raw[:, columns(h)] + jnp.exp(-rate_of(h) * (place + 1.0)) * fresh * x for h, x in zip(heads, cross)
            ]
            means = [jnp.mean(r * r, axis=-1, keepdims=True) for r in raws]
            outs = [
                (r * lax.rsqrt(m + 1e-06) * gain[pl.ds(h, 1), :]).astype(BF16) for r, m, h in zip(raws, means, heads)
            ]
            for x, h in zip(outs, heads):
                o_ref[:, columns(h)] = x

    loads[0].wait()
    loads[1].wait()
    pl.semaphore_wait(barrier, jnp.where(chip < chips - 1, 2, 1))
    flag_copy.start()
    loads[2].wait()
    loads[3].wait()

    def step_a(step, _):
        @pl.when(step < STEPS)
        def _():
            give_now = [state(theirs + g).astype(BF16) for g in pairs(step)]
            for g, a in zip(pairs(step), give_now):
                give[g] = a
            for g in pairs(step):
                give_copy(g).start()
            own_now = [state(mine + g) for g in pairs(step)]
            for g, b in zip(pairs(step), own_now):
                own[g] = b

        @pl.when(step == 1)
        def _():
            flag_copy.wait_recv()

        @pl.when((step >= 1) & (chip == 0))
        def _():
            chain(step - 1, True)

        return 0

    lax.fori_loop(0, STEPS + 1, step_a, 0)
    loads[4].wait()
    loads[5].wait()

    @pl.when(chip >= 2)
    def _():
        lax.fori_loop(0, STEPS, lambda step, _: (both(step), 0)[1], 0)

    def step_c(step, _):
        @pl.when((step < STEPS) & (chip > 0))
        def _():
            chain(step, False)

        @pl.when((step < STEPS) & (chip < 2))
        def _():
            both(step)

        @pl.when((step >= 1) & (chip != 1))
        def _():
            output(step - 1)

        return 0

    lax.fori_loop(0, STEPS + 1, step_c, 0)

    @pl.when(chip == 1)
    def _():
        lax.fori_loop(0, STEPS, lambda step, _: (output(step), 0)[1], 0)

    flag_copy.wait_send()

    def drain(g, _):
        give_copy(g).wait_send()
        pass_copy(g).wait_send()

        @pl.when(chip < chips - 1)
        def _():
            for p in range(PIECES):
                up_copy(g, p).wait_send()

        return 0

    lax.fori_loop(0, HALF, drain, 0)


def on_device(queries, keys, values, doc_starts, decay_exps, norm_gain):
    rows = queries.shape[0]
    chips = lax.axis_size("ctx") // 2
    vmem, hbm = (pl.BlockSpec(memory_space=m) for m in (pltpu.VMEM, pltpu.HBM))
    half = (HALF, HEAD, HEAD)
    sem = pltpu.SemaphoreType.DMA
    return pl.pallas_call(
        functools.partial(kernel, chips),
        out_shape=jax.ShapeDtypeStruct(queries.shape, BF16),
        in_specs=[hbm] * 6,
        out_specs=vmem,
        scratch_shapes=[
            pltpu.SMEM((HEADS,), jnp.int32),
            pltpu.VMEM((1, rows), jnp.int32),
            pltpu.VMEM((HEADS, HEAD), F32),
            *[pltpu.VMEM(queries.shape, BF16)] * 3,
            pltpu.VMEM(half, F32),
            *[pltpu.VMEM(half, BF16)] * 7,
            pltpu.VMEM(queries.shape, F32),
            pltpu.VMEM((8, HEAD), F32),
            pltpu.VMEM((8, HEAD), F32),
            sem((9,)),
            *[sem((HALF,))] * 2,
            *[sem((HALF * PIECES,))] * 2,
            *[sem((HALF,))] * 2,
            sem((1,)),
            sem((1,)),
        ],
        compiler_params=pltpu.CompilerParams(
            collective_id=0, has_side_effects=True, vmem_limit_bytes=32 * 2**20
        ),
        name="chain",
    )(
        *[
            pltpu.with_memory_space_constraint(a, pltpu.HBM)
            for a in (
                decay_exps,
                doc_starts.reshape(1, rows),
                norm_gain.reshape(HEADS, HEAD),
                queries, keys, values,
            )
        ]
    )


def solution(mesh):
    return jax.shard_map(
        on_device,
        mesh=mesh,
        in_specs=(
            P(("dp", "ctx"), None),
            P(("dp", "ctx"), None),
            P(("dp", "ctx"), None),
            P(("dp", "ctx")),
            P(),
            P(),
        ),
        out_specs=P(("dp", "ctx"), None),
        check_vma=False,
    )
```

```python
import functools

import jax
import jax.numpy as jnp
from jax import lax
from jax.experimental import pallas as pl
from jax.experimental.pallas import tpu as pltpu
from jax.sharding import PartitionSpec as P

HEADS = 32
HEAD = 128
HALF = HEADS // 2
UNROLL = 2
STEPS = HALF // UNROLL
PIECES = 2
PIECE = HEAD // PIECES
F32 = jnp.float32
BF16 = jnp.bfloat16
MESH = pl.DeviceIdType.MESH


def kernel(
    chips, exps_hbm, doc_hbm, gain_hbm, q_hbm, k_hbm, v_hbm, o_ref,
    exps, doc, gain, q, k, v, own, give, got, up_out, up_in, pass_out, pass_in, low, raw, flag_out, flag_in,
    load_sem, give_send, give_recv, up_send, up_recv, pass_send, pass_recv, flag_send, flag_recv,
):
    rows = q.shape[0]
    me = lax.axis_index("ctx")
    core, chip = lax.rem(me, 2), lax.div(me, 2)
    partner, above, below = me + 1 - 2 * core, me + 2, me - 2
    mine, theirs = core * HALF, (1 - core) * HALF

    def load(i, src, dst, first):
        cols = pl.ds(pl.multiple_of(first * HEAD, HALF * HEAD), HALF * HEAD)
        return pltpu.make_async_copy(src.at[:, cols], dst.at[:, cols], load_sem.at[i])

    loads = [
        load(0, k_hbm, k, theirs), load(1, v_hbm, v, theirs), load(2, k_hbm, k, mine),
        load(3, v_hbm, v, mine), load(4, q_hbm, q, mine), load(5, q_hbm, q, theirs),
    ]
    small = [
        pltpu.make_async_copy(src, dst, load_sem.at[6 + i])
        for i, (src, dst) in enumerate(((doc_hbm, doc), (exps_hbm, exps), (gain_hbm, gain)))
    ]
    for c in small + loads:
        c.start()

    barrier = pltpu.get_barrier_semaphore()
    pl.semaphore_signal(barrier, inc=1, device_id={"ctx": partner}, device_id_type=MESH)

    @pl.when(chip > 0)
    def _():
        pl.semaphore_signal(barrier, inc=1, device_id={"ctx": below}, device_id_type=MESH)

    for c in small:
        c.wait()
    starts = doc[...].astype(F32)
    sub = lax.broadcasted_iota(jnp.int32, (rows, rows), 0)
    lane = lax.broadcasted_iota(jnp.int32, (rows, rows), 1)
    wide = jnp.broadcast_to(starts, (rows, rows))
    count_col = jnp.sum(jnp.where(lane <= sub, wide, 0.0), axis=1, keepdims=True)
    start_col = jnp.sum(jnp.where(lane == sub, wide, 0.0), axis=1, keepdims=True)
    count_row = jnp.sum(jnp.where(sub <= lane, jnp.broadcast_to(start_col, (rows, rows)), 0.0), axis=0, keepdims=True)
    total = jnp.sum(starts, axis=1, keepdims=True)
    same = (count_col == count_row) & (sub >= lane)
    gaps = jnp.maximum(sub - lane, 0).astype(F32)
    place = lax.broadcasted_iota(jnp.int32, (rows, HEAD), 0).astype(F32)
    fresh = jnp.broadcast_to(jnp.where(count_col == 0.0, 1.0, 0.0), (rows, HEAD))
    trail = jnp.broadcast_to(jnp.where(count_col == total, 1.0, 0.0), (rows, HEAD))
    whole = jnp.where(total == 0.0, 1.0, 0.0)
    flag_out[...] = jnp.broadcast_to(whole, flag_out.shape)

    def columns(h):
        return pl.ds(pl.multiple_of(h * HEAD, HEAD), HEAD)

    def rate_of(h):
        return exps[h].astype(F32) * (1.0 / 65536.0)

    def state(h):
        scale = jnp.exp(-rate_of(h) * (rows - 1.0 - place)) * trail
        kd = (k[:, columns(h)].astype(F32) * scale).astype(BF16)
        return lax.dot_general(kd, v[:, columns(h)], (((0,), (0,)), ((), ())), preferred_element_type=F32)

    def remote(src, dst, ssem, rsem, dev):
        return pltpu.make_async_remote_copy(
            src_ref=src, dst_ref=dst, send_sem=ssem, recv_sem=rsem, device_id={"ctx": dev}, device_id_type=MESH
        )

    def give_copy(g):
        return remote(give.at[g], got.at[g], give_send.at[g], give_recv.at[g], partner)

    def up_copy(g, p):
        part = (g, pl.ds(p * PIECE, PIECE))
        i = g * PIECES + p
        return remote(up_out.at[part], up_in.at[part], up_send.at[i], up_recv.at[i], above)

    def pass_copy(g):
        return remote(pass_out.at[g], pass_in.at[g], pass_send.at[g], pass_recv.at[g], partner)

    flag_copy = remote(flag_out, flag_in, flag_send.at[0], flag_recv.at[0], partner)

    def chain(step, first, us=range(UNROLL)):
        at0 = core == 0
        for u in us:
            g = step * UNROLL + u
            give_copy(g).wait_recv()
            full = jnp.exp(jnp.full((1, HEAD), -rate_of(mine + g) * rows, F32))
            f_me, f_partner = full * flag_out[0:1, :], full * flag_in[0:1, :]
            f0, f1 = jnp.where(at0, f_me, f_partner), jnp.where(at0, f_partner, f_me)
            for p in range(PIECES):
                part = (g, pl.ds(p * PIECE, PIECE))
                held, other = own[part], got[part].astype(F32)
                s0, s1 = jnp.where(at0, held, other), jnp.where(at0, other, held)
                if first:
                    before = jnp.zeros((PIECE, HEAD), F32)
                    middle = s0
                else:
                    up_copy(g, p).wait_recv()
                    before = up_in[part].astype(F32)
                    middle = f0 * before + s0
                up_out[part] = (f1 * middle + s1).astype(BF16)

                @pl.when(chip < chips - 1)
                def _():
                    up_copy(g, p).start()

                pass_out[part] = jnp.where(at0, middle, before).astype(BF16)
                low[part] = jnp.where(at0, before, middle).astype(BF16)
            pass_copy(g).start()

    def pairs(step):
        return [step * UNROLL + u for u in range(UNROLL)]

    def both(step, sides):
        heads = [first + g for first in sides for g in pairs(step)]
        scores = [
            lax.dot_general(q[:, columns(h)], k[:, columns(h)], (((1,), (1,)), ((), ())), preferred_element_type=F32)
            for h in heads
        ]
        weighted = [
            (x * jnp.where(same, jnp.exp(-rate_of(h) * gaps), 0.0)).astype(BF16) for x, h in zip(scores, heads)
        ]
        sums = [jnp.dot(w, v[:, columns(h)], preferred_element_type=F32) for w, h in zip(weighted, heads)]
        for x, h in zip(sums, heads):
            raw[:, columns(h)] = x

    def output(step, own_side):
        for first, ref in [(mine, low)] if own_side else [(theirs, pass_in)]:
            heads = [first + g for g in pairs(step)]
            if ref is pass_in:
                for g in pairs(step):
                    pass_copy(g).wait_recv()
            carries = [ref[g] for g in pairs(step)]
            cross = [jnp.dot(q[:, columns(h)], c, preferred_element_type=F32) for h, c in zip(heads, carries)]
            raws = [
                raw[:, columns(h)] + jnp.exp(-rate_of(h) * (place + 1.0)) * fresh * x for h, x in zip(heads, cross)
            ]
            means = [jnp.mean(r * r, axis=-1, keepdims=True) for r in raws]
            outs = [
                (r * lax.rsqrt(m + 1e-06) * gain[pl.ds(h, 1), :]).astype(BF16) for r, m, h in zip(raws, means, heads)
            ]
            for x, h in zip(outs, heads):
                o_ref[:, columns(h)] = x

    loads[0].wait()
    loads[1].wait()
    pl.semaphore_wait(barrier, jnp.where(chip < chips - 1, 2, 1))
    flag_copy.start()
    loads[2].wait()
    loads[3].wait()

    def step_a(step, _):
        @pl.when(step < STEPS)
        def _():
            give_now = [state(theirs + g).astype(BF16) for g in pairs(step)]
            for g, a in zip(pairs(step), give_now):
                give[g] = a
            for g in pairs(step):
                give_copy(g).start()
            own_now = [state(mine + g) for g in pairs(step)]
            for g, b in zip(pairs(step), own_now):
                own[g] = b

        @pl.when(step == 1)
        def _():
            flag_copy.wait_recv()

        @pl.when((step >= 1) & (chip == 0))
        def _():
            chain(step - 1, True)

        return 0

    lax.fori_loop(0, STEPS + 1, step_a, 0)
    loads[4].wait()
    loads[5].wait()

    @pl.when(chip >= 2)
    def _():
        lax.fori_loop(0, STEPS, lambda step, _: (both(step, (mine, theirs)), 0)[1], 0)

    def step_c(step, _):
        for u, side in enumerate((mine, theirs)):
            @pl.when(chip > 0)
            def _():
                chain(step, False, (u,))

            @pl.when(chip < 2)
            def _():
                both(step, (side,))

            if u == 0:
                @pl.when((step >= 1) & (chip != 1))
                def _():
                    output(step - 1, False)
            else:
                @pl.when(chip != 1)
                def _():
                    output(step, True)

        return 0

    lax.fori_loop(0, STEPS, step_c, 0)

    @pl.when(chip != 1)
    def _():
        output(STEPS - 1, False)

    @pl.when(chip == 1)
    def _():
        lax.fori_loop(0, STEPS, lambda step, _: (output(step, True), output(step, False), 0)[2], 0)

    flag_copy.wait_send()

    def drain(g, _):
        give_copy(g).wait_send()
        pass_copy(g).wait_send()

        @pl.when(chip < chips - 1)
        def _():
            for p in range(PIECES):
                up_copy(g, p).wait_send()

        return 0

    lax.fori_loop(0, HALF, drain, 0)


def on_device(queries, keys, values, doc_starts, decay_exps, norm_gain):
    rows = queries.shape[0]
    chips = lax.axis_size("ctx") // 2
    vmem, hbm = (pl.BlockSpec(memory_space=m) for m in (pltpu.VMEM, pltpu.HBM))
    half = (HALF, HEAD, HEAD)
    sem = pltpu.SemaphoreType.DMA
    return pl.pallas_call(
        functools.partial(kernel, chips),
        out_shape=jax.ShapeDtypeStruct(queries.shape, BF16),
        in_specs=[hbm] * 6,
        out_specs=vmem,
        scratch_shapes=[
            pltpu.SMEM((HEADS,), jnp.int32),
            pltpu.VMEM((1, rows), jnp.int32),
            pltpu.VMEM((HEADS, HEAD), F32),
            *[pltpu.VMEM(queries.shape, BF16)] * 3,
            pltpu.VMEM(half, F32),
            *[pltpu.VMEM(half, BF16)] * 7,
            pltpu.VMEM(queries.shape, F32),
            pltpu.VMEM((8, HEAD), F32),
            pltpu.VMEM((8, HEAD), F32),
            sem((9,)),
            *[sem((HALF,))] * 2,
            *[sem((HALF * PIECES,))] * 2,
            *[sem((HALF,))] * 2,
            sem((1,)),
            sem((1,)),
        ],
        compiler_params=pltpu.CompilerParams(
            collective_id=0, has_side_effects=True, vmem_limit_bytes=32 * 2**20
        ),
        name="chain",
    )(
        *[
            pltpu.with_memory_space_constraint(a, pltpu.HBM)
            for a in (
                decay_exps,
                doc_starts.reshape(1, rows),
                norm_gain.reshape(HEADS, HEAD),
                queries, keys, values,
            )
        ]
    )


def solution(mesh):
    return jax.shard_map(
        on_device,
        mesh=mesh,
        in_specs=(
            P(("dp", "ctx"), None),
            P(("dp", "ctx"), None),
            P(("dp", "ctx"), None),
            P(("dp", "ctx")),
            P(),
            P(),
        ),
        out_specs=P(("dp", "ctx"), None),
        check_vma=False,
    )
```

```python
import functools

import jax
import jax.numpy as jnp
from jax import lax
from jax.experimental import pallas as pl
from jax.experimental.pallas import tpu as pltpu
from jax.sharding import PartitionSpec as P

HEADS = 32
HEAD = 128
HALF = HEADS // 2
UNROLL = 4
STEPS = HALF // UNROLL
PIECES = 2
PIECE = HEAD // PIECES
F32 = jnp.float32
BF16 = jnp.bfloat16
MESH = pl.DeviceIdType.MESH


def kernel(
    chips, exps_hbm, doc_hbm, gain_hbm, q_hbm, k_hbm, v_hbm, o_ref,
    exps, doc, gain, q, k, v, own, give, got, up_out, up_in, pass_out, pass_in, low, raw, flag_out, flag_in,
    load_sem, give_send, give_recv, up_send, up_recv, pass_send, pass_recv, flag_send, flag_recv,
):
    rows = q.shape[0]
    me = lax.axis_index("ctx")
    core, chip = lax.rem(me, 2), lax.div(me, 2)
    partner, above, below = me + 1 - 2 * core, me + 2, me - 2
    mine, theirs = core * HALF, (1 - core) * HALF

    def load(i, src, dst, first):
        cols = pl.ds(pl.multiple_of(first * HEAD, HALF * HEAD), HALF * HEAD)
        return pltpu.make_async_copy(src.at[:, cols], dst.at[:, cols], load_sem.at[i])

    loads = [
        load(0, k_hbm, k, theirs), load(1, v_hbm, v, theirs), load(2, k_hbm, k, mine),
        load(3, v_hbm, v, mine), load(4, q_hbm, q, mine), load(5, q_hbm, q, theirs),
    ]
    small = [
        pltpu.make_async_copy(src, dst, load_sem.at[6 + i])
        for i, (src, dst) in enumerate(((doc_hbm, doc), (exps_hbm, exps), (gain_hbm, gain)))
    ]
    for c in small + loads:
        c.start()

    barrier = pltpu.get_barrier_semaphore()
    pl.semaphore_signal(barrier, inc=1, device_id={"ctx": partner}, device_id_type=MESH)

    @pl.when(chip > 0)
    def _():
        pl.semaphore_signal(barrier, inc=1, device_id={"ctx": below}, device_id_type=MESH)

    for c in small:
        c.wait()
    starts = doc[...].astype(F32)
    sub = lax.broadcasted_iota(jnp.int32, (rows, rows), 0)
    lane = lax.broadcasted_iota(jnp.int32, (rows, rows), 1)
    wide = jnp.broadcast_to(starts, (rows, rows))
    count_col = jnp.sum(jnp.where(lane <= sub, wide, 0.0), axis=1, keepdims=True)
    start_col = jnp.sum(jnp.where(lane == sub, wide, 0.0), axis=1, keepdims=True)
    count_row = jnp.sum(jnp.where(sub <= lane, jnp.broadcast_to(start_col, (rows, rows)), 0.0), axis=0, keepdims=True)
    total = jnp.sum(starts, axis=1, keepdims=True)
    same = (count_col == count_row) & (sub >= lane)
    gaps = jnp.maximum(sub - lane, 0).astype(F32)
    place = lax.broadcasted_iota(jnp.int32, (rows, HEAD), 0).astype(F32)
    fresh = jnp.broadcast_to(jnp.where(count_col == 0.0, 1.0, 0.0), (rows, HEAD))
    trail = jnp.broadcast_to(jnp.where(count_col == total, 1.0, 0.0), (rows, HEAD))
    whole = jnp.where(total == 0.0, 1.0, 0.0)
    flag_out[...] = jnp.broadcast_to(whole, flag_out.shape)

    def columns(h):
        return pl.ds(pl.multiple_of(h * HEAD, HEAD), HEAD)

    def rate_of(h):
        return exps[h].astype(F32) * (1.0 / 65536.0)

    def state(h):
        scale = jnp.exp(-rate_of(h) * (rows - 1.0 - place)) * trail
        kd = (k[:, columns(h)].astype(F32) * scale).astype(BF16)
        return lax.dot_general(kd, v[:, columns(h)], (((0,), (0,)), ((), ())), preferred_element_type=F32)

    def remote(src, dst, ssem, rsem, dev):
        return pltpu.make_async_remote_copy(
            src_ref=src, dst_ref=dst, send_sem=ssem, recv_sem=rsem, device_id={"ctx": dev}, device_id_type=MESH
        )

    def give_copy(g):
        return remote(give.at[g], got.at[g], give_send.at[g], give_recv.at[g], partner)

    def up_copy(g, p):
        part = (g, pl.ds(p * PIECE, PIECE))
        i = g * PIECES + p
        return remote(up_out.at[part], up_in.at[part], up_send.at[i], up_recv.at[i], above)

    def pass_copy(g):
        return remote(pass_out.at[g], pass_in.at[g], pass_send.at[g], pass_recv.at[g], partner)

    flag_copy = remote(flag_out, flag_in, flag_send.at[0], flag_recv.at[0], partner)

    def chain(step, first):
        at0 = core == 0
        for u in range(UNROLL):
            g = step * UNROLL + u
            give_copy(g).wait_recv()
            full = jnp.exp(jnp.full((1, HEAD), -rate_of(mine + g) * rows, F32))
            f_me, f_partner = full * flag_out[0:1, :], full * flag_in[0:1, :]
            f0, f1 = jnp.where(at0, f_me, f_partner), jnp.where(at0, f_partner, f_me)
            for p in range(PIECES):
                part = (g, pl.ds(p * PIECE, PIECE))
                held, other = own[part], got[part].astype(F32)
                s0, s1 = jnp.where(at0, held, other), jnp.where(at0, other, held)
                if first:
                    before = jnp.zeros((PIECE, HEAD), F32)
                    middle = s0
                else:
                    up_copy(g, p).wait_recv()
                    before = up_in[part].astype(F32)
                    middle = f0 * before + s0
                up_out[part] = (f1 * middle + s1).astype(BF16)

                @pl.when(chip < chips - 1)
                def _():
                    up_copy(g, p).start()

                pass_out[part] = jnp.where(at0, middle, before).astype(BF16)
                low[part] = jnp.where(at0, before, middle).astype(BF16)
            pass_copy(g).start()

    def pairs(step):
        return [step * UNROLL + u for u in range(UNROLL)]

    def both(step):
        heads = [first + g for first in (mine, theirs) for g in pairs(step)]
        scores = [
            lax.dot_general(q[:, columns(h)], k[:, columns(h)], (((1,), (1,)), ((), ())), preferred_element_type=F32)
            for h in heads
        ]
        weighted = [
            (x * jnp.where(same, jnp.exp(-rate_of(h) * gaps), 0.0)).astype(BF16) for x, h in zip(scores, heads)
        ]
        sums = [jnp.dot(w, v[:, columns(h)], preferred_element_type=F32) for w, h in zip(weighted, heads)]
        for x, h in zip(sums, heads):
            raw[:, columns(h)] = x

    def output(step):
        for first, ref in ((mine, low), (theirs, pass_in)):
            heads = [first + g for g in pairs(step)]
            if ref is pass_in:
                for g in pairs(step):
                    pass_copy(g).wait_recv()
            carries = [ref[g] for g in pairs(step)]
            cross = [jnp.dot(q[:, columns(h)], c, preferred_element_type=F32) for h, c in zip(heads, carries)]
            raws = [
                raw[:, columns(h)] + jnp.exp(-rate_of(h) * (place + 1.0)) * fresh * x for h, x in zip(heads, cross)
            ]
            means = [jnp.mean(r * r, axis=-1, keepdims=True) for r in raws]
            outs = [
                (r * lax.rsqrt(m + 1e-06) * gain[pl.ds(h, 1), :]).astype(BF16) for r, m, h in zip(raws, means, heads)
            ]
            for x, h in zip(outs, heads):
                o_ref[:, columns(h)] = x

    loads[0].wait()
    loads[1].wait()
    pl.semaphore_wait(barrier, jnp.where(chip < chips - 1, 2, 1))
    flag_copy.start()
    loads[2].wait()
    loads[3].wait()

    def step_a(step, _):
        @pl.when(step < STEPS)
        def _():
            give_now = [state(theirs + g).astype(BF16) for g in pairs(step)]
            for g, a in zip(pairs(step), give_now):
                give[g] = a
            for g in pairs(step):
                give_copy(g).start()
            own_now = [state(mine + g) for g in pairs(step)]
            for g, b in zip(pairs(step), own_now):
                own[g] = b

        @pl.when(step == 1)
        def _():
            flag_copy.wait_recv()

        @pl.when((step >= 1) & (chip == 0))
        def _():
            chain(step - 1, True)

        return 0

    lax.fori_loop(0, STEPS + 1, step_a, 0)
    loads[4].wait()
    loads[5].wait()

    @pl.when(chip >= 2)
    def _():
        lax.fori_loop(0, STEPS, lambda step, _: (both(step), 0)[1], 0)

    def step_c(step, _):
        @pl.when((step < STEPS) & (chip > 0))
        def _():
            chain(step, False)

        @pl.when((step < STEPS) & (chip < 2))
        def _():
            both(step)

        @pl.when((step >= 1) & (chip != 1))
        def _():
            output(step - 1)

        return 0

    lax.fori_loop(0, STEPS + 1, step_c, 0)

    @pl.when(chip == 1)
    def _():
        lax.fori_loop(0, STEPS, lambda step, _: (output(step), 0)[1], 0)

    flag_copy.wait_send()

    def drain(g, _):
        give_copy(g).wait_send()
        pass_copy(g).wait_send()

        @pl.when(chip < chips - 1)
        def _():
            for p in range(PIECES):
                up_copy(g, p).wait_send()

        return 0

    lax.fori_loop(0, HALF, drain, 0)


def on_device(queries, keys, values, doc_starts, decay_exps, norm_gain):
    rows = queries.shape[0]
    chips = lax.axis_size("ctx") // 2
    vmem, hbm = (pl.BlockSpec(memory_space=m) for m in (pltpu.VMEM, pltpu.HBM))
    half = (HALF, HEAD, HEAD)
    sem = pltpu.SemaphoreType.DMA
    return pl.pallas_call(
        functools.partial(kernel, chips),
        out_shape=jax.ShapeDtypeStruct(queries.shape, BF16),
        in_specs=[hbm] * 6,
        out_specs=vmem,
        scratch_shapes=[
            pltpu.SMEM((HEADS,), jnp.int32),
            pltpu.VMEM((1, rows), jnp.int32),
            pltpu.VMEM((HEADS, HEAD), F32),
            *[pltpu.VMEM(queries.shape, BF16)] * 3,
            pltpu.VMEM(half, F32),
            *[pltpu.VMEM(half, BF16)] * 7,
            pltpu.VMEM(queries.shape, F32),
            pltpu.VMEM((8, HEAD), F32),
            pltpu.VMEM((8, HEAD), F32),
            sem((9,)),
            *[sem((HALF,))] * 2,
            *[sem((HALF * PIECES,))] * 2,
            *[sem((HALF,))] * 2,
            sem((1,)),
            sem((1,)),
        ],
        compiler_params=pltpu.CompilerParams(
            collective_id=0, has_side_effects=True, vmem_limit_bytes=32 * 2**20
        ),
        name="chain",
    )(
        *[
            pltpu.with_memory_space_constraint(a, pltpu.HBM)
            for a in (
                decay_exps,
                doc_starts.reshape(1, rows),
                norm_gain.reshape(HEADS, HEAD),
                queries, keys, values,
            )
        ]
    )


def solution(mesh):
    return jax.shard_map(
        on_device,
        mesh=mesh,
        in_specs=(
            P(("dp", "ctx"), None),
            P(("dp", "ctx"), None),
            P(("dp", "ctx"), None),
            P(("dp", "ctx")),
            P(),
            P(),
        ),
        out_specs=P(("dp", "ctx"), None),
        check_vma=False,
    )
```
